128 devices in a mesh: tb: 16 (over z_hi, y, core), ti: 8 (over z_lo, x).
Axes of the slice: x: 4, y: 4, z: 4 (z_hi: 2, z_lo: 2; z = z_hi * 2 + z_lo), core: 2. Of those that a mesh axis runs over, the one named last changes fastest.
Arguments:
- sources: float32 [256, 256, 512], P(('tb', 'ti')), may hold values from -4 to 4
- initial_state: float32 [256, 512], replicated, may hold values from -6 to 6
- roughness: float32 [256, 512], replicated, may hold values from 0.5 to 1
- region_ids: int32 [16, 16], replicated, may hold values from 0 to 15
- diffusion_table: float32 [16], replicated, may hold values from 0.02 to 0.1
- velocity_table: float32 [16, 2], replicated, may hold values from -0.05 to 0.05
Outputs:
- iterate: float32 [256, 256, 512], P(('tb', 'ti'))
The draws below stay inside these ranges and needn't reach their ends.
All inputs are finite; a program needn't handle non-finite values.
Results may differ from the reference program's by a relative error of at most 0.00002.
Values sent between devices are 32-bit elements; how exact they have to be, the bound alone decides.
A program may use at most 128 MiB of HBM per device.

```python
import jax
import jax.numpy as jnp
from jax import lax

NX = 256
NY = 512
REGIONS = 16
KINDS = 16
STEPS = 256


def with_ends(values, own_key, smallest, high):
    spot = [jax.random.randint(jax.random.fold_in(own_key, axis), (), 0, length) for axis, length in enumerate(values.shape)]
    longest = values.shape.index(max(values.shape))
    next_to = spot[:longest] + [(spot[longest] + 1) % values.shape[longest]] + spot[longest + 1:]
    return values.at[tuple(spot)].set(smallest).at[tuple(next_to)].set(high)


def block_scale(stream_key, shape, cuts, low, largest):
    factor_of = 1.0
    for dim, blocks in cuts:
        draws = jax.random.uniform(jax.random.fold_in(jax.random.fold_in(stream_key, 6), dim), (blocks,), jnp.float32, low / len(cuts), largest / len(cuts))
        factor_of = factor_of * jnp.repeat(jnp.exp(draws), shape[dim] // blocks).reshape((-1,) + (1,) * (len(shape) - 1 - dim))
    return factor_of


def noise(own_key, extent, deviation, reach, cuts=(), dtype=jnp.bfloat16):
    factor_of = block_scale(own_key, extent, cuts, -0.22, 0.18) if cuts else 1.0
    entries = jax.random.normal(own_key, extent, jnp.float32) * deviation * factor_of
    return jnp.minimum(jnp.maximum(entries, -reach), reach).astype(dtype)


def setup_inputs(seed: int = 0) -> dict:
    splits = jax.random.split(jax.random.key(seed), 7)
    return {
        "sources": noise(splits[0], (STEPS, NX, NY), 0.3, 4.0, ((0, 128),), jnp.float32),
        "initial_state": noise(splits[1], (NX, NY), 1.0, 6.0, (), jnp.float32),
        "roughness": jnp.clip(jax.random.uniform(splits[2], (NX, NY), jnp.float32, 0.5, 1.0), 0.5, 1.0),
        "region_ids": with_ends(jax.random.randint(splits[3], (REGIONS, REGIONS), 0, KINDS), jax.random.fold_in(splits[3], 1), 0, KINDS - 1).astype(jnp.int32),
        "diffusion_table": jnp.clip(jax.random.uniform(splits[4], (KINDS,), jnp.float32, 0.02, 0.1), 0.02, 0.1),
        "velocity_table": jnp.clip(jax.random.uniform(splits[5], (KINDS, 2), jnp.float32, -0.05, 0.05), -0.05, 0.05),
    }


def coefficients(region_ids, diffusion_table, velocity_table, roughness):
    width_x = roughness.shape[0] // region_ids.shape[0]
    width_y = roughness.shape[1] // region_ids.shape[1]

    def expand(lookup):
        return jnp.repeat(jnp.repeat(lookup, width_x, 0), width_y, 1)

    diffusion = expand(diffusion_table[region_ids]) * roughness
    speeds = velocity_table[region_ids]
    return (diffusion, expand(speeds[..., 0]), expand(speeds[..., 1]))


def coarsen(values):
    shape_now = values.shape
    blocked = values.reshape(shape_now[:-2] + (shape_now[-2] // 2, 2, shape_now[-1] // 2, 2))
    return blocked.mean(axis=(-3, -1))


def refine(values):
    return jnp.repeat(jnp.repeat(values, 2, -2), 2, -1)


def level_down(coef):
    return (coarsen(coef[0]), 2.0 * coarsen(coef[1]), 2.0 * coarsen(coef[2]))


def advance(state_now, diffusion, speed_x, speed_y):
    east_side = jnp.roll(state_now, -1, -2)
    west_side = jnp.roll(state_now, 1, -2)
    north_side = jnp.roll(state_now, -1, -1)
    south_side = jnp.roll(state_now, 1, -1)
    laplacian = east_side + west_side + north_side + south_side - 4.0 * state_now
    return (state_now + diffusion * laplacian
            - jnp.maximum(speed_x, 0.0) * (state_now - west_side)
            - jnp.minimum(speed_x, 0.0) * (east_side - state_now)
            - jnp.maximum(speed_y, 0.0) * (state_now - south_side)
            - jnp.minimum(speed_y, 0.0) * (north_side - state_now))


def sweep_grouped(start, grouped, coef):
    states = []
    current = start
    for offset in range(grouped.shape[1]):
        current = advance(current, *coef) + grouped[:, offset]
        states.append(current)
    return states


def reference(sources, initial_state, roughness, region_ids, diffusion_table, velocity_table):
    fine_coef = coefficients(region_ids, diffusion_table, velocity_table, roughness)
    middle_coef = level_down(fine_coef)
    coarse_coef = level_down(middle_coef)
    blocks = sources.shape[0] // 4
    grouped = sources.reshape((blocks, 4) + sources.shape[1:])
    zero_all = jnp.zeros((blocks,) + initial_state.shape, jnp.float32)
    first_pass = sweep_grouped(zero_all, grouped, fine_coef)
    c_first = first_pass[3]
    second_pass = sweep_grouped(jnp.concatenate([initial_state[None], c_first[:-1]]), grouped, fine_coef)
    residual_c = second_pass[3] - c_first
    rhs_middle = coarsen(residual_c)
    outer_count = blocks // 4
    mid_grouped = rhs_middle.reshape((outer_count, 4) + rhs_middle.shape[1:])
    zero_mid = jnp.zeros((outer_count,) + rhs_middle.shape[1:], jnp.float32)
    zero_one = jnp.zeros((1,) + rhs_middle.shape[1:], jnp.float32)
    mid_first = sweep_grouped(zero_mid, mid_grouped, middle_coef)
    mid_c = mid_first[3]
    coarse_rhs = coarsen(mid_c)

    def chain_step(state_now, rhs_now):
        new_state = advance(state_now, *coarse_coef) + rhs_now
        return new_state, new_state

    chain_zero = jnp.zeros(coarse_rhs.shape[1:], jnp.float32)
    _, chain_states = lax.scan(chain_step, chain_zero, coarse_rhs)
    mid_fixed = refine(chain_states)
    mid_last = sweep_grouped(jnp.concatenate([zero_one, mid_fixed[:-1]]), mid_grouped, middle_coef)
    correction = jnp.stack([mid_last[0], mid_last[1], mid_last[2], mid_fixed], 1)
    correction = correction.reshape((blocks,) + rhs_middle.shape[1:])
    c_fixed = c_first + refine(correction)
    last_pass = sweep_grouped(jnp.concatenate([initial_state[None], c_fixed[:-1]]), grouped, fine_coef)
    return jnp.stack([last_pass[0], last_pass[1], last_pass[2], c_fixed], 1).reshape(sources.shape)
```

```python
import functools

import jax
import jax.numpy as jnp
from jax import lax
from jax.experimental import pallas as pl
from jax.experimental.pallas import tpu as pltpu
from jax.sharding import PartitionSpec as P

MESH = pl.DeviceIdType.MESH
F32 = jnp.float32
BF16 = jnp.bfloat16
CHUNKS = 4


def wrap(ref, rows):
    ref[0] = pltpu.roll(ref[rows], 1, 0)
    ref[rows + 1] = pltpu.roll(ref[1], 7, 0)


def stencil(coef, r, centre, west, east):
    width = centre.shape[-1]
    south = pltpu.roll(centre, 1, 1)
    north = pltpu.roll(centre, width - 1, 1)
    return (
        (coef[0, r] * centre + coef[1, r] * west)
        + coef[2, r] * east
        + (coef[3, r] * south + coef[4, r] * north)
    )


def propagate(src, coef, rows, emit):
    wrap(src, rows)
    for r in range(rows):
        emit(r, stencil(coef, r, src[r + 1], src[r], src[r + 2]))


def into(dst):
    def emit(r, value):
        dst[r + 1] = value

    return emit


def exact_dot(x, matrix):
    first = x.astype(BF16)
    rest = x - first.astype(F32)
    second = rest.astype(BF16)
    third = (rest - second.astype(F32)).astype(BF16)

    def dot(part):
        return jnp.dot(part, matrix, preferred_element_type=F32)

    return dot(first) + (dot(second) + dot(third))


def pair_rows(value):
    rows, eight, width = value.shape
    halves = value.reshape(rows // 2, 2, eight, width)
    return halves[:, 0] + halves[:, 1]


def coarsen(value, matrix):
    rows, eight, width = value.shape
    summed = pair_rows(value).reshape(rows // 2 * eight, width)
    return exact_dot(summed, matrix).reshape(rows // 2, eight, width // 2)


def refine_lanes(value, matrix):
    rows, eight, width = value.shape
    return exact_dot(value.reshape(rows * eight, width), matrix).reshape(rows, eight, width * 2)


def put_refined(dst, value, matrix):
    wide = refine_lanes(value, matrix)
    for r in range(value.shape[0]):
        dst[2 * r + 1] = wide[r]
        dst[2 * r + 2] = wide[r]


def set_coefficients(coef, r, diffusion, speed_x, speed_y):
    coef[0, r] = 1.0 - 4.0 * diffusion - jnp.abs(speed_x) - jnp.abs(speed_y)
    coef[1, r] = diffusion + jnp.maximum(speed_x, 0.0)
    coef[2, r] = diffusion - jnp.minimum(speed_x, 0.0)
    coef[3, r] = diffusion + jnp.maximum(speed_y, 0.0)
    coef[4, r] = diffusion - jnp.minimum(speed_y, 0.0)


def block_matrix(rows, columns, wide_rows, entry):
    row = lax.broadcasted_iota(jnp.int32, (rows, columns), 0)
    column = lax.broadcasted_iota(jnp.int32, (rows, columns), 1)
    same = (row // 2 == column) if wide_rows else (row == column // 2)
    return jnp.where(same, entry, 0.0).astype(BF16)


def kernel(
    src, start, rough, ids, diffusion_table, velocity_table, out,
    raw, maps, ids_wide, coef0, coef1, coef2, down1, down2, up1, up0,
    rhs, y, work, tmid, c_own, y_in, c_in, third, beta, beta_in, mid_own, mid_in, level1, e_own, e_in, g_own, g_in,
    out_raw, in_sem, out_sem, y_send, y_recv, c_send, c_recv, b_send, b_recv, m_send, m_recv, e_send, e_recv, g_send, g_recv,
):
    tb, ti = lax.axis_index("tb"), lax.axis_index("ti")
    outer = lax.axis_size("tb")
    odd = lax.rem(ti, 2) == 1
    even = lax.rem(ti, 2) == 0
    slot = ti // 2
    first_interval = (tb == 0) & (slot == 0)
    last_interval = (tb == outer - 1) & (slot == 3)
    next_tb = lax.rem(tb + jnp.where(slot == 3, 1, 0), outer)
    next_even = lax.rem(ti - lax.rem(ti, 2) + 2, 8)
    width = 512

    barrier = pltpu.get_barrier_semaphore()
    for d in range(8):
        from_tb = lax.rem(tb + (outer - 1 if d >= 6 else 0), outer)

        @pl.when((from_tb != tb) | (ti != d))
        def _():
            pl.semaphore_signal(barrier, 1, device_id=(from_tb, d), device_id_type=MESH)

    @pl.when(ti == 7)
    def _():
        pl.semaphore_signal(barrier, 1, device_id=(tb, 6), device_id_type=MESH)

    for d in range(1, 16):

        @pl.when(tb - d >= 0)
        def _():
            pl.semaphore_signal(barrier, 1, device_id=(tb - d, ti), device_id_type=MESH)

    def load(index, array, part):
        return [
            pltpu.make_async_copy(
                array.at[:, pl.ds(128 * t, 128)] if part is None else array.at[part, :, pl.ds(128 * t, 128)],
                raw.at[index, t],
                in_sem.at[index, t],
            )
            for t in range(4)
        ]

    loads = [load(0, rough, None), load(1, src, 0), load(2, src, 1), load(3, start, None)]
    for group in loads:
        for copy in group:
            copy.start()

    def raw_row(index, r):
        return jnp.concatenate([raw[index, t, pl.ds(r, 8, stride=32), :] for t in range(4)], axis=1)

    down1[...] = block_matrix(512, 256, True, 0.25)
    down2[...] = block_matrix(256, 128, True, 0.25)
    up1[...] = block_matrix(128, 256, False, 1.0)
    up0[...] = block_matrix(256, 512, False, 1.0)

    ids_wide[...] = jnp.full(ids_wide.shape, -1, jnp.int32)
    ids_wide[:, 0:16] = ids[...]
    kinds = jnp.concatenate([ids_wide[pl.ds(h, 8, stride=2), :] for h in range(2)], axis=0)
    tables = [jnp.zeros(kinds.shape, F32) for _ in range(3)]
    for kind in range(16):
        hit = kinds == kind
        for which, entry in enumerate((diffusion_table[kind], velocity_table[kind, 0], velocity_table[kind, 1])):
            tables[which] = jnp.where(hit, entry, tables[which])

    def spread(cells, scale):
        column = lax.broadcasted_iota(jnp.int32, (128, 16 * cells), 0)
        cell = lax.broadcasted_iota(jnp.int32, (128, 16 * cells), 1)
        return jnp.where(cell // cells == column, scale, 0.0).astype(F32)

    stacked = jnp.concatenate(tables, axis=0)

    def expand(rows, cells, scale):
        return jnp.dot(rows, spread(cells, scale), precision=lax.Precision.HIGHEST, preferred_element_type=F32)

    maps[...] = expand(stacked, 32, 1.0)
    speeds1 = expand(stacked[16:], 16, 2.0)
    speeds2 = expand(stacked[16:], 8, 4.0)

    for copy in loads[0]:
        copy.wait()
    for r in range(32):
        h = r // 16
        diffusion = maps[8 * h : 8 * h + 8] * raw_row(0, r)
        tmid[r] = diffusion
        set_coefficients(coef0, r, diffusion, maps[16 + 8 * h : 24 + 8 * h], maps[32 + 8 * h : 40 + 8 * h])
    diffusion1 = coarsen(tmid[...], down1[...])
    for r in range(16):
        h = r // 8
        set_coefficients(coef1, r, diffusion1[r], speeds1[8 * h : 8 * h + 8], speeds1[16 + 8 * h : 24 + 8 * h])
    diffusion2 = coarsen(diffusion1, down2[...])
    for r in range(8):
        h = r // 4
        set_coefficients(coef2, r, diffusion2[r], speeds2[8 * h : 8 * h + 8], speeds2[16 + 8 * h : 24 + 8 * h])

    for group in loads[1:]:
        for copy in group:
            copy.wait()
    for r in range(32):
        rhs[0, r + 1] = raw_row(1, r)
        rhs[1, r + 1] = raw_row(2, r)

    def add_second(r, value):
        total = value + rhs[1, r + 1]
        y[r + 1] = total

    propagate(rhs.at[0], coef0, 32, add_second)

    pl.semaphore_wait(barrier, jnp.where(ti < 6, 7, jnp.where(ti == 6, 9, 8)) + outer - 1 - tb)

    chunk = 32 // CHUNKS

    def y_copy(c):
        return pltpu.make_async_remote_copy(
            src_ref=y.at[pl.ds(1 + c * chunk, chunk)],
            dst_ref=y_in.at[pl.ds(1 + c * chunk, chunk)],
            send_sem=y_send.at[c],
            recv_sem=y_recv.at[c],
            device_id=(tb, ti + 1),
            device_id_type=MESH,
        )

    @pl.when(even)
    def _():
        for c in range(CHUNKS):
            y_copy(c).start()

    for r in range(32):
        initial = raw_row(3, r)
        work[0, r + 1] = jnp.where(last_interval, jnp.where(odd, initial, 0.0), y[r + 1])

        @pl.when(first_interval)
        def _():
            c_in[r] = initial

    def turn(i, carry):
        propagate(work.at[lax.rem(i, 2)], coef0, 32, into(work.at[1 - lax.rem(i, 2)]))
        return carry

    lax.fori_loop(0, jnp.where(odd, 4, 6), turn, 0)
    beta[...] = coarsen(work[0, 1:33], down1[...])

    next_slot = lax.rem(slot + 1, 4)

    def beta_copy(target):
        return pltpu.make_async_remote_copy(
            src_ref=beta,
            dst_ref=beta_in.at[2 * next_slot + lax.rem(ti, 2)],
            send_sem=b_send.at[target],
            recv_sem=b_recv.at[2 * next_slot + lax.rem(ti, 2)],
            device_id=(next_tb, 2 * target + 1),
            device_id_type=MESH,
        )

    for target in range(3):

        @pl.when(next_slot <= target)
        def _():
            beta_copy(target).start()

    def level1_turn(i, carry):
        propagate(level1.at[lax.rem(i, 2)], coef1, 16, into(level1.at[1 - lax.rem(i, 2)]))
        return carry

    level1[0, 1:17] = beta[...]
    count = 3 - next_slot
    lax.fori_loop(0, count, level1_turn, 0)
    e_own[...] = coarsen(level1[lax.rem(count, 2), 1:17], down2[...])

    def e_copy(target):
        return pltpu.make_async_remote_copy(
            src_ref=e_own,
            dst_ref=e_in.at[ti],
            send_sem=e_send.at[target],
            recv_sem=e_recv.at[ti],
            device_id=(next_tb, target),
            device_id_type=MESH,
        )

    for target in range(8):

        @pl.when((ti != target) | (next_tb != tb))
        def _():
            e_copy(target).start()

        @pl.when((ti == target) & (next_tb == tb))
        def _():
            e_in[target] = e_own[...]

    def e_arrival(source):
        return pltpu.make_async_remote_copy(
            src_ref=e_own,
            dst_ref=e_in.at[source],
            send_sem=e_send.at[source],
            recv_sem=e_recv.at[source],
            device_id=(tb, source),
            device_id_type=MESH,
        )

    for source in range(8):

        @pl.when((ti != source) | (source >= 6))
        def _():
            e_arrival(source).wait_recv()

    total = e_in[0]
    for source in range(1, 8):
        total = total + e_in[source]
    g_own[...] = total

    def g_copy(d):
        return pltpu.make_async_remote_copy(
            src_ref=g_own,
            dst_ref=g_in.at[tb],
            send_sem=g_send.at[d],
            recv_sem=g_recv.at[tb],
            device_id=(tb + d, ti),
            device_id_type=MESH,
        )

    for d in range(1, 16):

        @pl.when(tb + d < outer)
        def _():
            g_copy(d).start()

    def c_copy(c, target):
        return pltpu.make_async_remote_copy(
            src_ref=c_own.at[pl.ds(c * chunk, chunk)],
            dst_ref=c_in.at[pl.ds(c * chunk, chunk)],
            send_sem=c_send.at[2 * c + target],
            recv_sem=c_recv.at[c],
            device_id=(next_tb, next_even + target),
            device_id_type=MESH,
        )

    def mid_copy(target):
        return pltpu.make_async_remote_copy(
            src_ref=mid_own,
            dst_ref=mid_in,
            send_sem=m_send.at[target],
            recv_sem=m_recv,
            device_id=(tb, next_even + target),
            device_id_type=MESH,
        )

    def beta_arrival(which):
        return pltpu.make_async_remote_copy(
            src_ref=beta,
            dst_ref=beta_in.at[which],
            send_sem=b_send.at[0],
            recv_sem=b_recv.at[which],
            device_id=(tb, ti - 1),
            device_id_type=MESH,
        )

    @pl.when(odd)
    def _():
        for c in range(CHUNKS):
            y_copy(c).wait_recv()

        def emit_first(r, value):
            work[0, r + 1] = value
            third[r] = value + rhs[0, r + 1]

        propagate(y_in, coef0, 32, emit_first)

        def emit_second(r, value):
            c_own[r] = value + y[r + 1]

        propagate(work.at[0], coef0, 32, emit_second)

        @pl.when(jnp.logical_not(last_interval))
        def _():
            for c in range(CHUNKS):
                for target in range(2):
                    c_copy(c, target).start()

    @pl.when(odd & (slot < 3))
    def _():
        for which in range(2):
            beta_arrival(which).wait_recv()
        level1[0, 1:17] = beta_in[0] + beta_in[1]

        def mid_turn(i, carry):
            for which in range(2):
                beta_arrival(2 * i + which).wait_recv()

            def emit(r, value):
                level1[lax.rem(i, 2), r + 1] = value + (beta_in[2 * i, r] + beta_in[2 * i + 1, r])

            propagate(level1.at[lax.rem(i + 1, 2)], coef1, 16, emit)
            return carry

        lax.fori_loop(1, slot + 1, mid_turn, 0)
        mid_own[...] = level1[lax.rem(slot, 2), 1:17]
        for target in range(2):
            mid_copy(target).start()

    @pl.when(slot == 0)
    def _():
        mid_in[...] = jnp.zeros(mid_in.shape, F32)

    def level2(value):
        first = pltpu.roll(value[7], 1, 0)
        last = pltpu.roll(value[0], 7, 0)
        rows = [first] + [value[r] for r in range(8)] + [last]
        return jnp.stack([stencil(coef2, r, rows[r + 1], rows[r], rows[r + 2]) for r in range(8)])

    def g_arrival(source):
        return pltpu.make_async_remote_copy(
            src_ref=g_own,
            dst_ref=g_in.at[source],
            send_sem=g_send.at[0],
            recv_sem=g_recv.at[source],
            device_id=(0, ti),
            device_id_type=MESH,
        )

    def chain_turn(source, state):
        g_arrival(source).wait_recv()
        return level2(state) + g_in[source]

    before = lax.fori_loop(0, tb, chain_turn, jnp.zeros((8, 8, 128), F32))
    g_in[tb] = level2(before) + g_own[...]

    put_refined(level1.at[0], before, up1[...])
    lax.fori_loop(0, slot, level1_turn, 0)
    here = lax.rem(slot, 2)

    @pl.when(slot > 0)
    def _():
        mid_copy(0).wait_recv()

    @pl.when(jnp.logical_not(first_interval))
    def _():
        for c in range(CHUNKS):
            c_copy(c, 0).wait_recv()

    wide = refine_lanes(level1[here, 1:17] + mid_in[...], up0[...])
    for r in range(32):
        work[0, r + 1] = c_in[r] + wide[r // 2]

    def put_out(index, r, value):
        for t in range(4):
            out_raw[index, t, pl.ds(r, 8, stride=32), :] = value[:, 128 * t : 128 * t + 128]

    def out_copies(index):
        return [
            pltpu.make_async_copy(out_raw.at[index, t], out.at[index, :, pl.ds(128 * t, 128)], out_sem.at[index, t])
            for t in range(4)
        ]

    @pl.when(even)
    def _():
        def emit_first(r, value):
            state = value + rhs[0, r + 1]
            work[1, r + 1] = state
            put_out(0, r, state)

        propagate(work.at[0], coef0, 32, emit_first)
        for copy in out_copies(0):
            copy.start()

        def emit_second(r, value):
            put_out(1, r, value + rhs[1, r + 1])

        propagate(work.at[1], coef0, 32, emit_second)

    @pl.when(odd)
    def _():
        propagate(work.at[0], coef0, 32, into(work.at[1]))
        propagate(work.at[1], coef0, 32, into(work.at[0]))

        def emit(r, value):
            put_out(0, r, value + third[r])

        propagate(work.at[0], coef0, 32, emit)
        for copy in out_copies(0):
            copy.start()

        @pl.when(slot < 3)
        def _():
            def emit_end(r, value):
                mid_own_end[r] = value + mid_own[r]

            mid_own_end = beta_in.at[7]
            propagate(level1.at[here], coef1, 16, emit_end)

        @pl.when(slot == 3)
        def _():
            fixed = refine_lanes(g_in[tb], up1[...])
            for r in range(16):
                beta_in[7, r] = fixed[r // 2]

        wide = refine_lanes(beta_in[7], up0[...])
        for r in range(32):
            put_out(1, r, c_own[r] + wide[r // 2])

    for copy in out_copies(1):
        copy.start()

    @pl.when(even)
    def _():
        for c in range(CHUNKS):
            y_copy(c).wait_send()

    for target in range(3):

        @pl.when(next_slot <= target)
        def _():
            beta_copy(target).wait_send()

    for target in range(8):

        @pl.when((ti != target) | (next_tb != tb))
        def _():
            e_copy(target).wait_send()

    for d in range(1, 16):

        @pl.when(tb + d < outer)
        def _():
            g_copy(d).wait_send()

    @pl.when(odd & jnp.logical_not(last_interval))
    def _():
        for c in range(CHUNKS):
            for target in range(2):
                c_copy(c, target).wait_send()

    @pl.when(odd & (slot < 3))
    def _():
        for target in range(2):
            mid_copy(target).wait_send()

    for index in range(2):
        for copy in out_copies(index):
            copy.wait()


def shards(sources, initial_state, roughness, region_ids, diffusion_table, velocity_table):
    vmem, sems = pltpu.VMEM, pltpu.SemaphoreType.DMA
    scratch = dict(
        raw=vmem((4, 4, 256, 128), F32),
        maps=vmem((48, 512), F32),
        ids_wide=vmem((16, 128), jnp.int32),
        coef0=vmem((5, 32, 8, 512), F32),
        coef1=vmem((5, 16, 8, 256), F32),
        coef2=vmem((5, 8, 8, 128), F32),
        down1=vmem((512, 256), BF16),
        down2=vmem((256, 128), BF16),
        up1=vmem((128, 256), BF16),
        up0=vmem((256, 512), BF16),
        rhs=vmem((2, 34, 8, 512), F32),
        y=vmem((34, 8, 512), F32),
        work=vmem((2, 34, 8, 512), F32),
        tmid=vmem((32, 8, 512), F32),
        c_own=vmem((32, 8, 512), F32),
        y_in=vmem((34, 8, 512), F32),
        c_in=vmem((32, 8, 512), F32),
        third=vmem((32, 8, 512), F32),
        beta=vmem((16, 8, 256), F32),
        beta_in=vmem((8, 16, 8, 256), F32),
        mid_own=vmem((16, 8, 256), F32),
        mid_in=vmem((16, 8, 256), F32),
        level1=vmem((2, 18, 8, 256), F32),
        e_own=vmem((8, 8, 128), F32),
        e_in=vmem((8, 8, 8, 128), F32),
        g_own=vmem((8, 8, 128), F32),
        g_in=vmem((16, 8, 8, 128), F32),
        out_raw=vmem((2, 4, 256, 128), F32),
        in_sem=sems((4, 4)),
        out_sem=sems((2, 4)),
        y_send=sems((CHUNKS,)),
        y_recv=sems((CHUNKS,)),
        c_send=sems((2 * CHUNKS,)),
        c_recv=sems((CHUNKS,)),
        b_send=sems((3,)),
        b_recv=sems((8,)),
        m_send=sems((2,)),
        m_recv=sems(()),
        e_send=sems((8,)),
        e_recv=sems((8,)),
        g_send=sems((16,)),
        g_recv=sems((16,)),
    )
    anywhere = pl.BlockSpec(memory_space=pl.ANY)
    small = pl.BlockSpec(memory_space=pltpu.SMEM)
    return pl.pallas_call(
        kernel,
        out_shape=jax.ShapeDtypeStruct(sources.shape, F32),
        in_specs=[anywhere, anywhere, anywhere, pl.BlockSpec(memory_space=pltpu.VMEM), small, small],
        out_specs=anywhere,
        scratch_shapes=list(scratch.values()),
        compiler_params=pltpu.CompilerParams(
            collective_id=0, has_side_effects=True, vmem_limit_bytes=48 * 1024 * 1024
        ),
    )(sources, initial_state, roughness, region_ids, diffusion_table, velocity_table)


def solution(mesh):
    in_specs = (P(("tb", "ti"), None, None), P(), P(), P(), P(), P())
    out_specs = P(("tb", "ti"), None, None)
    return jax.shard_map(shards, mesh=mesh, in_specs=in_specs, out_specs=out_specs, check_vma=False)
```

```python
import functools

import jax
import jax.numpy as jnp
from jax import lax
from jax.experimental import pallas as pl
from jax.experimental.pallas import tpu as pltpu
from jax.sharding import PartitionSpec as P

MESH = pl.DeviceIdType.MESH
F32 = jnp.float32
BF16 = jnp.bfloat16

Y_CUTS = (0, 4, 8, 12, 16, 20, 24, 28, 32)
PIECES = len(Y_CUTS) - 1
C_PIECES = ((2, 6), (6, 10), (10, 14), (14, 18), (18, 22), (22, 26), (26, 32), (0, 2))
C_AFTER = (1, 2, 3, 4, 5, 6, 7, 7)
E_AFTER = 2


def wrap(ref, rows):
    ref[0] = pltpu.roll(ref[rows], 1, 0)
    ref[rows + 1] = pltpu.roll(ref[1], 7, 0)


def stencil(coef, r, centre, west, east):
    width = centre.shape[-1]
    south = pltpu.roll(centre, 1, 1)
    north = pltpu.roll(centre, width - 1, 1)
    return (
        (coef[0, r] * centre + coef[1, r] * west)
        + coef[2, r] * east
        + (coef[3, r] * south + coef[4, r] * north)
    )


def propagate(src, coef, rows, emit):
    wrap(src, rows)
    for r in range(rows):
        emit(r, stencil(coef, r, src[r + 1], src[r], src[r + 2]))


def into(dst):
    def emit(r, value):
        dst[r + 1] = value

    return emit


def exact_dot(x, matrix):
    first = x.astype(BF16)
    rest = x - first.astype(F32)
    second = rest.astype(BF16)
    third = (rest - second.astype(F32)).astype(BF16)

    def dot(part):
        return jnp.dot(part, matrix, preferred_element_type=F32)

    return dot(first) + (dot(second) + dot(third))


def pair_rows(value):
    rows, eight, width = value.shape
    halves = value.reshape(rows // 2, 2, eight, width)
    return halves[:, 0] + halves[:, 1]


def coarsen(value, matrix):
    rows, eight, width = value.shape
    summed = pair_rows(value).reshape(rows // 2 * eight, width)
    return exact_dot(summed, matrix).reshape(rows // 2, eight, width // 2)


def refine_lanes(value, matrix):
    rows, eight, width = value.shape
    return exact_dot(value.reshape(rows * eight, width), matrix).reshape(rows, eight, width * 2)


def put_refined(dst, value, matrix):
    wide = refine_lanes(value, matrix)
    for r in range(value.shape[0]):
        dst[2 * r + 1] = wide[r]
        dst[2 * r + 2] = wide[r]


def set_coefficients(coef, r, diffusion, speed_x, speed_y):
    coef[0, r] = 1.0 - 4.0 * diffusion - jnp.abs(speed_x) - jnp.abs(speed_y)
    coef[1, r] = diffusion + jnp.maximum(speed_x, 0.0)
    coef[2, r] = diffusion - jnp.minimum(speed_x, 0.0)
    coef[3, r] = diffusion + jnp.maximum(speed_y, 0.0)
    coef[4, r] = diffusion - jnp.minimum(speed_y, 0.0)


def block_matrix(rows, columns, wide_rows, entry):
    row = lax.broadcasted_iota(jnp.int32, (rows, columns), 0)
    column = lax.broadcasted_iota(jnp.int32, (rows, columns), 1)
    same = (row // 2 == column) if wide_rows else (row == column // 2)
    return jnp.where(same, entry, 0.0).astype(BF16)


def kernel(
    src, start, rough, ids, diffusion_table, velocity_table, out,
    raw, ids_raw, diffusion_entries, velocity_entries, maps, ids_wide, coef0, coef1, coef2, down1, down2, up1, up0,
    rhs, y, work, tmid, c_own, y_in, c_in, third, beta, swap_in, b_own, b_in, mid, mid_own, level1, e_own, e_in, g_own, g_in,
    out_raw, in_sem, small_sem, out_sem, y_send, y_recv, c_send, c_recv, s_send, s_recv, b_send, b_recv,
    e_send, e_recv, g_send, g_recv,
):
    tb, ti = lax.axis_index("tb"), lax.axis_index("ti")
    outer = lax.axis_size("tb")
    parity = lax.rem(ti, 2)
    odd = parity == 1
    even = parity == 0
    slot = ti // 2
    first_interval = (tb == 0) & (slot == 0)
    last_interval = (tb == outer - 1) & (slot == 3)
    next_tb = lax.rem(tb + jnp.where(slot == 3, 1, 0), outer)
    next_even = lax.rem(ti - parity + 2, 8)
    next_slot = lax.rem(slot + 1, 4)
    partner = ti + 1 - 2 * parity

    def load(index, array, part):
        return [
            pltpu.make_async_copy(
                array.at[:, pl.ds(128 * t, 128)] if part is None else array.at[part, :, pl.ds(128 * t, 128)],
                raw.at[index, t],
                in_sem.at[index, t],
            )
            for t in range(4)
        ]

    small = [
        pltpu.make_async_copy(ids, ids_raw, small_sem.at[0]),
        pltpu.make_async_copy(diffusion_table, diffusion_entries, small_sem.at[1]),
        pltpu.make_async_copy(velocity_table, velocity_entries, small_sem.at[2]),
    ]
    load_rough, load_first, load_second, load_start = load(0, rough, None), load(1, src, 0), load(2, src, 1), load(3, start, None)
    for copy in small + load_rough + load_first + load_second:
        copy.start()

    @pl.when(first_interval | last_interval)
    def _():
        for copy in load_start:
            copy.start()

    barrier = pltpu.get_barrier_semaphore()
    for d in range(1, 16):

        @pl.when(tb - d >= 0)
        def _():
            pl.semaphore_signal(barrier, 1, device_id=(tb - d, ti), device_id_type=MESH)

    for d in range(8):
        from_tb = lax.rem(tb + (outer - 1 if d >= 6 else 0), outer)

        @pl.when((from_tb != tb) | (ti != d))
        def _():
            pl.semaphore_signal(barrier, 1, device_id=(from_tb, d), device_id_type=MESH)

    @pl.when(ti >= 6)
    def _():
        pl.semaphore_signal(barrier, 1, device_id=(tb, partner), device_id_type=MESH)

    def raw_row(index, r):
        return jnp.concatenate([raw[index, t, pl.ds(r, 8, stride=32), :] for t in range(4)], axis=1)

    down1[...] = block_matrix(512, 256, True, 0.25)
    down2[...] = block_matrix(256, 128, True, 0.25)
    up1[...] = block_matrix(128, 256, False, 1.0)
    up0[...] = block_matrix(256, 512, False, 1.0)

    for copy in small:
        copy.wait()
    ids_wide[...] = jnp.full(ids_wide.shape, -1, jnp.int32)
    ids_wide[:, 0:16] = ids_raw[...]
    kinds = jnp.concatenate([ids_wide[pl.ds(h, 8, stride=2), :] for h in range(2)], axis=0)
    tables = [jnp.zeros(kinds.shape, F32) for _ in range(3)]
    for kind in range(16):
        hit = kinds == kind
        entries = (diffusion_entries[kind], velocity_entries[0, kind], velocity_entries[1, kind])
        for which in range(3):
            tables[which] = jnp.where(hit, entries[which], tables[which])

    def spread(cells, scale):
        column = lax.broadcasted_iota(jnp.int32, (128, 16 * cells), 0)
        cell = lax.broadcasted_iota(jnp.int32, (128, 16 * cells), 1)
        return jnp.where(cell // cells == column, scale, 0.0).astype(F32)

    stacked = jnp.concatenate(tables, axis=0)

    def expand(rows, cells, scale):
        return jnp.dot(rows, spread(cells, scale), precision=lax.Precision.HIGHEST, preferred_element_type=F32)

    maps[...] = expand(stacked, 32, 1.0)
    speeds1 = expand(stacked[16:], 16, 2.0)
    speeds2 = expand(stacked[16:], 8, 4.0)

    for copy in load_rough:
        copy.wait()
    for r in range(32):
        h = r // 16
        diffusion = maps[8 * h : 8 * h + 8] * raw_row(0, r)
        tmid[r] = diffusion
        set_coefficients(coef0, r, diffusion, maps[16 + 8 * h : 24 + 8 * h], maps[32 + 8 * h : 40 + 8 * h])

    for copy in load_first + load_second:
        copy.wait()
    for r in range(32):
        rhs[0, r + 1] = raw_row(1, r)
        rhs[1, r + 1] = raw_row(2, r)

    def add_second(r, value):
        total = value + rhs[1, r + 1]
        y[r + 1] = total
        work[0, r + 1] = total

    propagate(rhs.at[0], coef0, 32, add_second)

    @pl.when(first_interval | last_interval)
    def _():
        for copy in load_start:
            copy.wait()

    @pl.when(first_interval)
    def _():
        for r in range(32):
            c_in[r] = raw_row(3, r)

    @pl.when(last_interval)
    def _():
        for r in range(32):
            work[0, r + 1] = jnp.where(odd, raw_row(3, r), 0.0)

    def turn(i, carry):
        propagate(work.at[lax.rem(i, 2)], coef0, 32, into(work.at[1 - lax.rem(i, 2)]))
        return carry

    lax.fori_loop(0, jnp.where(odd, 4, 6), turn, 0)
    beta[...] = coarsen(work[0, 1:33], down1[...])

    diffusion1 = coarsen(tmid[...], down1[...])
    for r in range(16):
        h = r // 8
        set_coefficients(coef1, r, diffusion1[r], speeds1[8 * h : 8 * h + 8], speeds1[16 + 8 * h : 24 + 8 * h])
    diffusion2 = coarsen(diffusion1, down2[...])
    for r in range(8):
        h = r // 4
        set_coefficients(coef2, r, diffusion2[r], speeds2[8 * h : 8 * h + 8], speeds2[16 + 8 * h : 24 + 8 * h])

    def level1_turn(i, carry):
        propagate(level1.at[lax.rem(i, 2)], coef1, 16, into(level1.at[1 - lax.rem(i, 2)]))
        return carry

    level1[0, 1:17] = beta[...]
    count = 3 - next_slot
    lax.fori_loop(0, count, level1_turn, 0)
    e_own[...] = coarsen(level1[lax.rem(count, 2), 1:17], down2[...])

    pl.semaphore_wait(barrier, jnp.where(ti < 6, 7, 9) + outer - 1 - tb)

    def e_copy(target):
        return pltpu.make_async_remote_copy(
            src_ref=e_own,
            dst_ref=e_in.at[ti],
            send_sem=e_send.at[target],
            recv_sem=e_recv.at[ti],
            device_id=(next_tb, target),
            device_id_type=MESH,
        )

    for target in range(8):

        @pl.when((ti != target) | (next_tb != tb))
        def _():
            e_copy(target).start()

        @pl.when((ti == target) & (next_tb == tb))
        def _():
            e_in[target] = e_own[...]

    swap = pltpu.make_async_remote_copy(
        src_ref=beta.at[pl.ds(8 - 8 * parity, 8)],
        dst_ref=swap_in,
        send_sem=s_send,
        recv_sem=s_recv,
        device_id=(tb, partner),
        device_id_type=MESH,
    )
    swap.start()

    def y_copy(piece):
        low, high = Y_CUTS[piece], Y_CUTS[piece + 1]
        return pltpu.make_async_remote_copy(
            src_ref=y.at[pl.ds(1 + low, high - low)],
            dst_ref=y_in.at[pl.ds(1 + low, high - low)],
            send_sem=y_send.at[piece],
            recv_sem=y_recv.at[piece],
            device_id=(tb, partner),
            device_id_type=MESH,
        )

    @pl.when(even)
    def _():
        for piece in range(PIECES):
            y_copy(piece).start()

    def b_copy(target):
        return pltpu.make_async_remote_copy(
            src_ref=b_own,
            dst_ref=b_in.at[next_slot, pl.ds(8 * parity, 8)],
            send_sem=b_send.at[target],
            recv_sem=b_recv.at[2 * next_slot + parity],
            device_id=(next_tb, target),
            device_id_type=MESH,
        )

    def b_arrival(which, half):
        return pltpu.make_async_remote_copy(
            src_ref=b_own,
            dst_ref=b_in.at[which, pl.ds(8 * half, 8)],
            send_sem=b_send.at[0],
            recv_sem=b_recv.at[2 * which + half],
            device_id=(tb, partner),
            device_id_type=MESH,
        )

    swap.wait_recv()
    b_own[...] = beta[pl.ds(8 * parity, 8)] + swap_in[...]
    for target in range(1, 8):

        @pl.when((next_slot < 3) & (target >= 2 * next_slot + 1))
        def _():
            b_copy(target).start()

    def c_copy(piece, target):
        low, high = C_PIECES[piece]
        return pltpu.make_async_remote_copy(
            src_ref=c_own.at[pl.ds(low, high - low)],
            dst_ref=c_in.at[pl.ds(low, high - low)],
            send_sem=c_send.at[2 * piece + target],
            recv_sem=c_recv.at[piece],
            device_id=(next_tb, next_even + target),
            device_id_type=MESH,
        )

    def first_step(r):
        value = stencil(coef0, r, y_in[r + 1], y_in[r], y_in[r + 2])
        work[0, r + 1] = value
        third[r] = value + rhs[0, r + 1]

    def second_step(r):
        c_own[r] = stencil(coef0, r, work[0, r + 1], work[0, r], work[0, r + 2]) + y[r + 1]

    def end_state(piece):
        y_copy(piece).wait_recv()
        low, high = Y_CUTS[piece], Y_CUTS[piece + 1]
        if piece == PIECES - 1:
            wrap(y_in, 32)
        for r in range(max(low - 1, 1), 32 if high == 32 else high - 1):
            first_step(r)
        if high == 32:
            first_step(0)
            wrap(work.at[0], 32)
        for which, (begin, end) in enumerate(C_PIECES):
            if C_AFTER[which] != piece:
                continue
            for r in range(begin, end):
                second_step(r)

            @pl.when(jnp.logical_not(last_interval))
            def _():
                for target in (1, 0):
                    c_copy(which, target).start()

    @pl.when(odd)
    def _():
        for piece in range(E_AFTER):
            end_state(piece)

    def e_arrival(source):
        return pltpu.make_async_remote_copy(
            src_ref=e_own,
            dst_ref=e_in.at[source],
            send_sem=e_send.at[source],
            recv_sem=e_recv.at[source],
            device_id=(tb, source),
            device_id_type=MESH,
        )

    for source in range(8):

        @pl.when((ti != source) | (source >= 6))
        def _():
            e_arrival(source).wait_recv()

    total = e_in[0]
    for source in range(1, 8):
        total = total + e_in[source]
    g_own[...] = total

    def g_copy(d):
        return pltpu.make_async_remote_copy(
            src_ref=g_own,
            dst_ref=g_in.at[tb],
            send_sem=g_send.at[d],
            recv_sem=g_recv.at[tb],
            device_id=(tb + d, ti),
            device_id_type=MESH,
        )

    for d in range(1, 16):

        @pl.when(tb + d < outer)
        def _():
            g_copy(d).start()

    @pl.when(odd)
    def _():
        for piece in range(E_AFTER, PIECES):
            end_state(piece)

    def mid_turn(i, carry):
        for half in range(2):
            b_arrival(i, half).wait_recv()

        def emit(r, value):
            level1[1 - lax.rem(i, 2), r + 1] = value + b_in[i, r]

        propagate(level1.at[lax.rem(i, 2)], coef1, 16, emit)
        return carry

    level1[0] = jnp.zeros(level1.shape[1:], F32)
    lax.fori_loop(0, slot, mid_turn, 0)
    mid[...] = level1[lax.rem(slot, 2), 1:17]

    @pl.when(odd & (slot < 3))
    def _():
        mid_turn(slot, 0)
        mid_own[...] = level1[1 - lax.rem(slot, 2), 1:17]

    def level2(value):
        first = pltpu.roll(value[7], 1, 0)
        last = pltpu.roll(value[0], 7, 0)
        rows = [first] + [value[r] for r in range(8)] + [last]
        return jnp.stack([stencil(coef2, r, rows[r + 1], rows[r], rows[r + 2]) for r in range(8)])

    def g_arrival(source):
        return pltpu.make_async_remote_copy(
            src_ref=g_own,
            dst_ref=g_in.at[source],
            send_sem=g_send.at[0],
            recv_sem=g_recv.at[source],
            device_id=(0, ti),
            device_id_type=MESH,
        )

    def chain_turn(source, state):
        g_arrival(source).wait_recv()
        return level2(state) + g_in[source]

    before = lax.fori_loop(0, tb, chain_turn, jnp.zeros((8, 8, 128), F32))
    g_in[tb] = level2(before) + g_own[...]

    put_refined(level1.at[0], before, up1[...])
    lax.fori_loop(0, slot, level1_turn, 0)
    here = lax.rem(slot, 2)
    wide = refine_lanes(level1[here, 1:17] + mid[...], up0[...])

    @pl.when(jnp.logical_not(first_interval))
    def _():
        for piece in range(len(C_PIECES)):
            c_copy(piece, 0).wait_recv()

    for r in range(32):
        work[0, r + 1] = c_in[r] + wide[r // 2]

    def put_out(index, r, value):
        for t in range(4):
            out_raw[index, t, pl.ds(r, 8, stride=32), :] = value[:, 128 * t : 128 * t + 128]

    def out_copies(index):
        return [
            pltpu.make_async_copy(out_raw.at[index, t], out.at[index, :, pl.ds(128 * t, 128)], out_sem.at[index, t])
            for t in range(4)
        ]

    @pl.when(even)
    def _():
        def emit_first(r, value):
            state = value + rhs[0, r + 1]
            work[1, r + 1] = state
            put_out(0, r, state)

        propagate(work.at[0], coef0, 32, emit_first)
        for copy in out_copies(0):
            copy.start()

        def emit_second(r, value):
            put_out(1, r, value + rhs[1, r + 1])

        propagate(work.at[1], coef0, 32, emit_second)

    @pl.when(odd)
    def _():
        @pl.when(slot < 3)
        def _():
            def emit_end(r, value):
                mid_own[r] = value + mid_own[r]

            propagate(level1.at[here], coef1, 16, emit_end)

        @pl.when(slot == 3)
        def _():
            fixed = refine_lanes(g_in[tb], up1[...])
            for r in range(16):
                mid_own[r] = fixed[r // 2]

        wide = refine_lanes(mid_own[...], up0[...])
        for r in range(32):
            put_out(1, r, c_own[r] + wide[r // 2])
        for copy in out_copies(1):
            copy.start()
        propagate(work.at[0], coef0, 32, into(work.at[1]))
        propagate(work.at[1], coef0, 32, into(work.at[0]))

        def emit(r, value):
            put_out(0, r, value + third[r])

        propagate(work.at[0], coef0, 32, emit)
        for copy in out_copies(0):
            copy.start()

    @pl.when(even)
    def _():
        for copy in out_copies(1):
            copy.start()

    swap.wait_send()

    @pl.when(even)
    def _():
        for piece in range(PIECES):
            y_copy(piece).wait_send()

    for target in range(1, 8):

        @pl.when((next_slot < 3) & (target >= 2 * next_slot + 1))
        def _():
            b_copy(target).wait_send()

    for target in range(8):

        @pl.when((ti != target) | (next_tb != tb))
        def _():
            e_copy(target).wait_send()

    for d in range(1, 16):

        @pl.when(tb + d < outer)
        def _():
            g_copy(d).wait_send()

    @pl.when(odd & jnp.logical_not(last_interval))
    def _():
        for piece in range(len(C_PIECES)):
            for target in range(2):
                c_copy(piece, target).wait_send()

    for index in range(2):
        for copy in out_copies(index):
            copy.wait()


def shards(sources, initial_state, roughness, region_ids, diffusion_table, velocity_table):
    vmem, sems = pltpu.VMEM, pltpu.SemaphoreType.DMA
    scratch = dict(
        raw=vmem((4, 4, 256, 128), F32),
        ids_raw=vmem((16, 16), jnp.int32),
        diffusion_entries=pltpu.SMEM((16,), F32),
        velocity_entries=pltpu.SMEM((2, 16), F32),
        maps=vmem((48, 512), F32),
        ids_wide=vmem((16, 128), jnp.int32),
        coef0=vmem((5, 32, 8, 512), F32),
        coef1=vmem((5, 16, 8, 256), F32),
        coef2=vmem((5, 8, 8, 128), F32),
        down1=vmem((512, 256), BF16),
        down2=vmem((256, 128), BF16),
        up1=vmem((128, 256), BF16),
        up0=vmem((256, 512), BF16),
        rhs=vmem((2, 34, 8, 512), F32),
        y=vmem((34, 8, 512), F32),
        work=vmem((2, 34, 8, 512), F32),
        tmid=vmem((32, 8, 512), F32),
        c_own=vmem((32, 8, 512), F32),
        y_in=vmem((34, 8, 512), F32),
        c_in=vmem((32, 8, 512), F32),
        third=vmem((32, 8, 512), F32),
        beta=vmem((16, 8, 256), F32),
        swap_in=vmem((8, 8, 256), F32),
        b_own=vmem((8, 8, 256), F32),
        b_in=vmem((3, 16, 8, 256), F32),
        mid=vmem((16, 8, 256), F32),
        mid_own=vmem((16, 8, 256), F32),
        level1=vmem((2, 18, 8, 256), F32),
        e_own=vmem((8, 8, 128), F32),
        e_in=vmem((8, 8, 8, 128), F32),
        g_own=vmem((8, 8, 128), F32),
        g_in=vmem((16, 8, 8, 128), F32),
        out_raw=vmem((2, 4, 256, 128), F32),
        in_sem=sems((4, 4)),
        small_sem=sems((3,)),
        out_sem=sems((2, 4)),
        y_send=sems((PIECES,)),
        y_recv=sems((PIECES,)),
        c_send=sems((2 * len(C_PIECES),)),
        c_recv=sems((len(C_PIECES),)),
        s_send=sems(()),
        s_recv=sems(()),
        b_send=sems((8,)),
        b_recv=sems((6,)),
        e_send=sems((8,)),
        e_recv=sems((8,)),
        g_send=sems((16,)),
        g_recv=sems((16,)),
    )
    anywhere = pl.BlockSpec(memory_space=pl.ANY)
    return pl.pallas_call(
        kernel,
        out_shape=pltpu.VMEM(sources.shape, F32),
        in_specs=[pl.BlockSpec(memory_space=pltpu.HBM)] * 6,
        out_specs=anywhere,
        scratch_shapes=list(scratch.values()),
        compiler_params=pltpu.CompilerParams(
            collective_id=0, has_side_effects=True, vmem_limit_bytes=60 * 1024 * 1024
        ),
    )(sources, initial_state, roughness, region_ids, diffusion_table, velocity_table.T)


def solution(mesh):
    in_specs = (P(("tb", "ti"), None, None), P(), P(), P(), P(), P())
    out_specs = P(("tb", "ti"), None, None)
    return jax.shard_map(shards, mesh=mesh, in_specs=in_specs, out_specs=out_specs, check_vma=False)
```

```python
import functools

import jax
import jax.numpy as jnp
from jax import lax
from jax.experimental import pallas as pl
from jax.experimental.pallas import tpu as pltpu
from jax.sharding import PartitionSpec as P

MESH = pl.DeviceIdType.MESH
F32 = jnp.float32
BF16 = jnp.bfloat16

Y_CUTS = (0, 4, 8, 12, 16, 20, 24, 28, 32)
PIECES = len(Y_CUTS) - 1
C_PIECES = ((2, 6), (6, 10), (10, 14), (14, 18), (18, 22), (22, 26), (26, 32), (0, 2))
C_AFTER = (1, 2, 3, 4, 5, 6, 7, 7)
E_AFTER = 2
EARLY_TURNS = 1
Y_EARLY = 2


def wrap(ref, rows):
    ref[0] = pltpu.roll(ref[rows], 1, 0)
    ref[rows + 1] = pltpu.roll(ref[1], 7, 0)


def stencil(coef, r, centre, west, east):
    width = centre.shape[-1]
    south = pltpu.roll(centre, 1, 1)
    north = pltpu.roll(centre, width - 1, 1)
    return (
        (coef[0, r] * centre + coef[1, r] * west)
        + coef[2, r] * east
        + (coef[3, r] * south + coef[4, r] * north)
    )


def propagate(src, coef, rows, emit):
    wrap(src, rows)
    for r in range(rows):
        emit(r, stencil(coef, r, src[r + 1], src[r], src[r + 2]))


def into(dst):
    def emit(r, value):
        dst[r + 1] = value

    return emit


def exact_dot(x, matrix):
    first = x.astype(BF16)
    rest = x - first.astype(F32)
    second = rest.astype(BF16)
    third = (rest - second.astype(F32)).astype(BF16)

    def dot(part):
        return jnp.dot(part, matrix, preferred_element_type=F32)

    return dot(first) + (dot(second) + dot(third))


def pair_rows(value):
    rows, eight, width = value.shape
    halves = value.reshape(rows // 2, 2, eight, width)
    return halves[:, 0] + halves[:, 1]


def coarsen(value, matrix):
    rows, eight, width = value.shape
    summed = pair_rows(value).reshape(rows // 2 * eight, width)
    return exact_dot(summed, matrix).reshape(rows // 2, eight, width // 2)


def refine_lanes(value, matrix):
    rows, eight, width = value.shape
    return exact_dot(value.reshape(rows * eight, width), matrix).reshape(rows, eight, width * 2)


def put_refined(dst, value, matrix):
    wide = refine_lanes(value, matrix)
    for r in range(value.shape[0]):
        dst[2 * r + 1] = wide[r]
        dst[2 * r + 2] = wide[r]


def set_coefficients(coef, r, diffusion, speed_x, speed_y):
    coef[0, r] = 1.0 - 4.0 * diffusion - jnp.abs(speed_x) - jnp.abs(speed_y)
    coef[1, r] = diffusion + jnp.maximum(speed_x, 0.0)
    coef[2, r] = diffusion - jnp.minimum(speed_x, 0.0)
    coef[3, r] = diffusion + jnp.maximum(speed_y, 0.0)
    coef[4, r] = diffusion - jnp.minimum(speed_y, 0.0)


def block_matrix(rows, columns, wide_rows, entry):
    row = lax.broadcasted_iota(jnp.int32, (rows, columns), 0)
    column = lax.broadcasted_iota(jnp.int32, (rows, columns), 1)
    same = (row // 2 == column) if wide_rows else (row == column // 2)
    return jnp.where(same, entry, 0.0).astype(BF16)


def kernel(
    src, start, rough, ids, diffusion_table, velocity_table, out,
    raw, ids_raw, diffusion_entries, velocity_entries, maps, ids_wide, coef0, coef1, coef2, down1, down2, up1, up0,
    rhs, y, work, tmid, c_own, y_in, c_in, third, beta, swap_in, b_own, b_in, mid, mid_own, level1, e_own, e_in, g_own, g_in,
    out_raw, in_sem, small_sem, out_sem, y_send, y_recv, c_send, c_recv, s_send, s_recv, b_send, b_recv,
    e_send, e_recv, g_send, g_recv, start_beta, start_e, start_e_send, start_b_send, ready_far, ready_all,
    states, w_send, w_recv,
):
    tb, ti = lax.axis_index("tb"), lax.axis_index("ti")
    outer = lax.axis_size("tb")
    parity = lax.rem(ti, 2)
    odd = parity == 1
    even = parity == 0
    slot = ti // 2
    first_interval = (tb == 0) & (slot == 0)
    last_interval = (tb == outer - 1) & (slot == 3)
    has_next = jnp.logical_not(last_interval)
    start_share = (tb == 0) & (slot == 3)
    next_tb = lax.rem(tb + jnp.where(slot == 3, 1, 0), outer)
    next_even = lax.rem(ti - parity + 2, 8)
    next_slot = lax.rem(slot + 1, 4)
    partner = ti + 1 - 2 * parity

    def load(index, array, part):
        return [
            pltpu.make_async_copy(
                array.at[:, pl.ds(128 * t, 128)] if part is None else array.at[part, :, pl.ds(128 * t, 128)],
                raw.at[index, t],
                in_sem.at[index, t],
            )
            for t in range(4)
        ]

    small = [
        pltpu.make_async_copy(ids, ids_raw, small_sem.at[0]),
        pltpu.make_async_copy(diffusion_table, diffusion_entries, small_sem.at[1]),
        pltpu.make_async_copy(velocity_table, velocity_entries, small_sem.at[2]),
    ]
    load_rough, load_first, load_second, load_start = load(0, rough, None), load(1, src, 0), load(2, src, 1), load(3, start, None)
    for copy in small + load_rough + load_first + load_second:
        copy.start()

    @pl.when(first_interval | start_share)
    def _():
        for copy in load_start:
            copy.start()

    barrier = pltpu.get_barrier_semaphore()

    def greet(to_tb, to_ti):
        pl.semaphore_signal(barrier, 1, device_id=(to_tb, to_ti), device_id_type=MESH)

    def across(bits):
        return tb + sum((bit - 2 * bit * lax.rem(tb // bit, 2)) for bit in bits)

    @pl.when(even)
    def _():
        for bits in ((1,), (2,), (4,), (2, 4), (8,)):
            greet(across(bits), ti)

    for d in range(1, 8):
        greet(tb, lax.rem(ti + d, 8))

    @pl.when(tb > 0)
    def _():
        for d in (6, 7):
            greet(tb - 1, d)

    def raw_row(index, r):
        return jnp.concatenate([raw[index, t, pl.ds(r, 8, stride=32), :] for t in range(4)], axis=1)

    down1[...] = block_matrix(512, 256, True, 0.25)
    down2[...] = block_matrix(256, 128, True, 0.25)
    up1[...] = block_matrix(128, 256, False, 1.0)
    up0[...] = block_matrix(256, 512, False, 1.0)

    for copy in small:
        copy.wait()
    ids_wide[...] = jnp.full(ids_wide.shape, -1, jnp.int32)
    ids_wide[:, 0:16] = ids_raw[...]
    kinds = jnp.concatenate([ids_wide[pl.ds(h, 8, stride=2), :] for h in range(2)], axis=0)
    tables = [jnp.zeros(kinds.shape, F32) for _ in range(3)]
    for kind in range(16):
        hit = kinds == kind
        entries = (diffusion_entries[kind], velocity_entries[0, kind], velocity_entries[1, kind])
        for which in range(3):
            tables[which] = jnp.where(hit, entries[which], tables[which])

    def spread(cells, scale):
        column = lax.broadcasted_iota(jnp.int32, (128, 16 * cells), 0)
        cell = lax.broadcasted_iota(jnp.int32, (128, 16 * cells), 1)
        return jnp.where(cell // cells == column, scale, 0.0).astype(F32)

    stacked = jnp.concatenate(tables, axis=0)

    def expand(rows, cells, scale):
        return jnp.dot(rows, spread(cells, scale), precision=lax.Precision.HIGHEST, preferred_element_type=F32)

    maps[...] = expand(stacked, 32, 1.0)
    speeds1 = expand(stacked[16:], 16, 2.0)
    speeds2 = expand(stacked[16:], 8, 4.0)

    for copy in load_rough:
        copy.wait()
    for r in range(32):
        h = r // 16
        diffusion = maps[8 * h : 8 * h + 8] * raw_row(0, r)
        tmid[r] = diffusion
        set_coefficients(coef0, r, diffusion, maps[16 + 8 * h : 24 + 8 * h], maps[32 + 8 * h : 40 + 8 * h])

    for copy in load_first + load_second:
        copy.wait()
    for r in range(32):
        rhs[0, r + 1] = raw_row(1, r)
        rhs[1, r + 1] = raw_row(2, r)

    def add_second(r, value):
        total = value + rhs[1, r + 1]
        y[r + 1] = total
        work[0, r + 1] = total

    propagate(rhs.at[0], coef0, 32, add_second)

    diffusion1 = coarsen(tmid[...], down1[...])
    for r in range(16):
        h = r // 8
        set_coefficients(coef1, r, diffusion1[r], speeds1[8 * h : 8 * h + 8], speeds1[16 + 8 * h : 24 + 8 * h])
    diffusion2 = coarsen(diffusion1, down2[...])
    for r in range(8):
        h = r // 4
        set_coefficients(coef2, r, diffusion2[r], speeds2[8 * h : 8 * h + 8], speeds2[16 + 8 * h : 24 + 8 * h])

    def y_copy(piece):
        low, high = Y_CUTS[piece], Y_CUTS[piece + 1]
        return pltpu.make_async_remote_copy(
            src_ref=y.at[pl.ds(1 + low, high - low)],
            dst_ref=y_in.at[pl.ds(1 + low, high - low)],
            send_sem=y_send.at[piece],
            recv_sem=y_recv.at[piece],
            device_id=(tb, partner),
            device_id_type=MESH,
        )

    def turn(i, carry):
        propagate(work.at[lax.rem(i, 2)], coef0, 32, into(work.at[1 - lax.rem(i, 2)]))
        return carry

    def level1_turn(i, carry):
        propagate(level1.at[lax.rem(i, 2)], coef1, 16, into(level1.at[1 - lax.rem(i, 2)]))
        return carry

    @pl.when(first_interval | start_share)
    def _():
        for copy in load_start:
            copy.wait()

    @pl.when(first_interval)
    def _():
        for r in range(32):
            c_in[r] = raw_row(3, r)

    @pl.when(start_share)
    def _():
        for r in range(32):
            work[0, r + 1] = raw_row(3, r)
        lax.fori_loop(0, 4, turn, 0)
        start_beta[...] = coarsen(work[0, 1:33], down1[...])
        level1[0, 1:17] = start_beta[...]
        lax.fori_loop(0, 3, level1_turn, 0)
        start_e[...] = coarsen(level1[1, 1:17], down2[...])
        for r in range(32):
            work[0, r + 1] = y[r + 1]

    lax.fori_loop(0, EARLY_TURNS, turn, 0)

    pl.semaphore_wait(barrier, 7 + jnp.where(even, 5, 0) + jnp.where((ti >= 6) & (tb < outer - 1), 8, 0))

    @pl.when(even)
    def _():
        pl.semaphore_signal(ready_far, 1, device_id=(across((8,)), ti), device_id_type=MESH)


    @pl.when(even)
    def _():
        for piece in range(Y_EARLY):
            y_copy(piece).start()

    def start_e_copy(target):
        return pltpu.make_async_remote_copy(
            src_ref=start_e,
            dst_ref=e_in.at[7],
            send_sem=start_e_send.at[target],
            recv_sem=e_recv.at[7],
            device_id=(tb, target),
            device_id_type=MESH,
        )

    def start_b_copy(target):
        return pltpu.make_async_remote_copy(
            src_ref=start_beta.at[pl.ds(8 * parity, 8)],
            dst_ref=b_in.at[0, pl.ds(8 * parity, 8)],
            send_sem=start_b_send.at[target],
            recv_sem=b_recv.at[parity],
            device_id=(tb, target),
            device_id_type=MESH,
        )

    @pl.when(start_share & odd)
    def _():
        for target in range(0, 8, 2):
            start_e_copy(target).start()

    @pl.when(start_share)
    def _():
        b_in[0, pl.ds(8 * parity, 8)] = start_beta[pl.ds(8 * parity, 8)]
        for target in range(1, 8):

            @pl.when(ti != target)
            def _():
                start_b_copy(target).start()

    @pl.when(tb == 0)
    def _():
        e_in[6] = jnp.zeros(e_own.shape, F32)

    lax.fori_loop(EARLY_TURNS, jnp.where(odd, 4, 6), turn, 0)
    beta[...] = coarsen(work[0, 1:33], down1[...])

    level1[0, 1:17] = beta[...]
    count = 3 - next_slot
    lax.fori_loop(0, count, level1_turn, 0)
    e_own[...] = coarsen(level1[lax.rem(count, 2), 1:17], down2[...])

    def e_copy(target):
        return pltpu.make_async_remote_copy(
            src_ref=e_own,
            dst_ref=e_in.at[ti],
            send_sem=e_send.at[target],
            recv_sem=e_recv.at[ti],
            device_id=(next_tb, target),
            device_id_type=MESH,
        )

    for target in range(0, 8, 2):

        @pl.when(has_next & ((ti != target) | (slot == 3)))
        def _():
            e_copy(target).start()

        @pl.when((ti == target) & (slot < 3))
        def _():
            e_in[target] = e_own[...]

    swap = pltpu.make_async_remote_copy(
        src_ref=beta.at[pl.ds(8 - 8 * parity, 8)],
        dst_ref=swap_in,
        send_sem=s_send,
        recv_sem=s_recv,
        device_id=(tb, partner),
        device_id_type=MESH,
    )
    swap.start()

    def b_copy(target):
        return pltpu.make_async_remote_copy(
            src_ref=b_own,
            dst_ref=b_in.at[next_slot, pl.ds(8 * parity, 8)],
            send_sem=b_send.at[target],
            recv_sem=b_recv.at[2 * next_slot + parity],
            device_id=(next_tb, target),
            device_id_type=MESH,
        )

    def b_arrival(which, half):
        return pltpu.make_async_remote_copy(
            src_ref=b_own,
            dst_ref=b_in.at[which, pl.ds(8 * half, 8)],
            send_sem=b_send.at[0],
            recv_sem=b_recv.at[2 * which + half],
            device_id=(tb, partner),
            device_id_type=MESH,
        )

    @pl.when(even)
    def _():
        for piece in range(Y_EARLY, PIECES):
            y_copy(piece).start()

    @pl.when(even)
    def _():
        pl.semaphore_wait(ready_far, 1)
        pl.semaphore_signal(ready_all, 1, device_id=(across((1,)), ti), device_id_type=MESH)

    swap.wait_recv()
    b_own[...] = beta[pl.ds(8 * parity, 8)] + swap_in[...]
    for target in range(1, 8):

        @pl.when(has_next & (next_slot < 3) & (target >= 2 * next_slot + 1))
        def _():
            b_copy(target).start()

    def c_copy(piece, target):
        low, high = C_PIECES[piece]
        return pltpu.make_async_remote_copy(
            src_ref=c_own.at[pl.ds(low, high - low)],
            dst_ref=c_in.at[pl.ds(low, high - low)],
            send_sem=c_send.at[2 * piece + target],
            recv_sem=c_recv.at[piece],
            device_id=(next_tb, next_even + target),
            device_id_type=MESH,
        )

    def first_step(r):
        value = stencil(coef0, r, y_in[r + 1], y_in[r], y_in[r + 2])
        work[0, r + 1] = value
        third[r] = value + rhs[0, r + 1]

    def second_step(r):
        c_own[r] = stencil(coef0, r, work[0, r + 1], work[0, r], work[0, r + 2]) + y[r + 1]

    def end_state(piece):
        y_copy(piece).wait_recv()
        low, high = Y_CUTS[piece], Y_CUTS[piece + 1]
        if piece == PIECES - 1:
            wrap(y_in, 32)
        for r in range(max(low - 1, 1), 32 if high == 32 else high - 1):
            first_step(r)
        if high == 32:
            first_step(0)
            wrap(work.at[0], 32)
        for which, (begin, end) in enumerate(C_PIECES):
            if C_AFTER[which] != piece:
                continue
            for r in range(begin, end):
                second_step(r)

            @pl.when(jnp.logical_not(last_interval))
            def _():
                for target in (1, 0):
                    c_copy(which, target).start()

    @pl.when(odd)
    def _():
        for piece in range(E_AFTER):
            end_state(piece)

    def e_arrival(source):
        return pltpu.make_async_remote_copy(
            src_ref=e_own,
            dst_ref=e_in.at[source],
            send_sem=e_send.at[source],
            recv_sem=e_recv.at[source],
            device_id=(tb, source),
            device_id_type=MESH,
        )

    def g_copy(d):
        return pltpu.make_async_remote_copy(
            src_ref=g_own,
            dst_ref=g_in.at[tb],
            send_sem=g_send.at[d],
            recv_sem=g_recv.at[tb],
            device_id=(tb + d, ti),
            device_id_type=MESH,
        )

    @pl.when(even)
    def _():
        for source in range(8):

            @pl.when((ti != source) if source < 6 else ((tb > 0) | (source == 7)))
            def _():
                e_arrival(source).wait_recv()

        total = e_in[0]
        for source in range(1, 8):
            total = total + e_in[source]
        g_own[...] = total

        pl.semaphore_wait(ready_all, 1)
        for d in range(1, 16):

            @pl.when(tb + d < outer)
            def _():
                g_copy(d).start()

    @pl.when(odd)
    def _():
        for piece in range(E_AFTER, PIECES):
            end_state(piece)

    def mid_turn(i, carry):
        for half in range(2):

            @pl.when((i > 0) | (tb > 0) | (ti != 6 + half))
            def _():
                b_arrival(i, half).wait_recv()

        def emit(r, value):
            level1[1 - lax.rem(i, 2), r + 1] = value + b_in[i, r]

        propagate(level1.at[lax.rem(i, 2)], coef1, 16, emit)
        return carry

    level1[0] = jnp.zeros(level1.shape[1:], F32)
    lax.fori_loop(0, slot, mid_turn, 0)
    mid[...] = level1[lax.rem(slot, 2), 1:17]

    @pl.when(odd & (slot < 3))
    def _():
        mid_turn(slot, 0)
        mid_own[...] = level1[1 - lax.rem(slot, 2), 1:17]

    def level2(value):
        first = pltpu.roll(value[7], 1, 0)
        last = pltpu.roll(value[0], 7, 0)
        rows = [first] + [value[r] for r in range(8)] + [last]
        return jnp.stack([stencil(coef2, r, rows[r + 1], rows[r], rows[r + 2]) for r in range(8)])

    def g_arrival(source):
        return pltpu.make_async_remote_copy(
            src_ref=g_own,
            dst_ref=g_in.at[source],
            send_sem=g_send.at[0],
            recv_sem=g_recv.at[source],
            device_id=(0, ti),
            device_id_type=MESH,
        )

    def chain_turn(source, state):
        g_arrival(source).wait_recv()
        return level2(state) + g_in[source]

    def state_copy(which):
        return pltpu.make_async_remote_copy(
            src_ref=states.at[which],
            dst_ref=states.at[which],
            send_sem=w_send.at[which],
            recv_sem=w_recv.at[which],
            device_id=(tb, partner),
            device_id_type=MESH,
        )

    @pl.when(even)
    def _():
        before = lax.fori_loop(0, tb, chain_turn, jnp.zeros((8, 8, 128), F32))
        states[0] = before
        state_copy(0).start()

        @pl.when(slot == 3)
        def _():
            states[1] = level2(before) + g_own[...]
            state_copy(1).start()

    @pl.when(odd)
    def _():
        state_copy(0).wait_recv()

    put_refined(level1.at[0], states[0], up1[...])
    lax.fori_loop(0, slot, level1_turn, 0)
    here = lax.rem(slot, 2)
    wide = refine_lanes(level1[here, 1:17] + mid[...], up0[...])

    def put_out(index, r, value):
        for t in range(4):
            out_raw[index, t, pl.ds(r, 8, stride=32), :] = value[:, 128 * t : 128 * t + 128]

    def out_copies(index):
        return [
            pltpu.make_async_copy(out_raw.at[index, t], out.at[index, :, pl.ds(128 * t, 128)], out_sem.at[index, t])
            for t in range(4)
        ]

    @pl.when(odd)
    def _():
        @pl.when(slot < 3)
        def _():
            def emit_end(r, value):
                mid_own[r] = value + mid_own[r]

            propagate(level1.at[here], coef1, 16, emit_end)

        @pl.when(slot == 3)
        def _():
            state_copy(1).wait_recv()
            fixed = refine_lanes(states[1], up1[...])
            for r in range(16):
                mid_own[r] = fixed[r // 2]

        wide_end = refine_lanes(mid_own[...], up0[...])
        for r in range(32):
            put_out(1, r, c_own[r] + wide_end[r // 2])
        for copy in out_copies(1):
            copy.start()

    @pl.when(jnp.logical_not(first_interval))
    def _():
        for piece in range(len(C_PIECES)):
            c_copy(piece, 0).wait_recv()

    for r in range(32):
        work[0, r + 1] = c_in[r] + wide[r // 2]

    @pl.when(even)
    def _():
        def emit_first(r, value):
            state = value + rhs[0, r + 1]
            work[1, r + 1] = state
            put_out(0, r, state)

        propagate(work.at[0], coef0, 32, emit_first)
        for copy in out_copies(0):
            copy.start()

        def emit_second(r, value):
            put_out(1, r, value + rhs[1, r + 1])

        propagate(work.at[1], coef0, 32, emit_second)

    @pl.when(odd)
    def _():
        propagate(work.at[0], coef0, 32, into(work.at[1]))
        propagate(work.at[1], coef0, 32, into(work.at[0]))

        def emit(r, value):
            put_out(0, r, value + third[r])

        propagate(work.at[0], coef0, 32, emit)
        for copy in out_copies(0):
            copy.start()

    @pl.when(even)
    def _():
        for copy in out_copies(1):
            copy.start()

    swap.wait_send()

    @pl.when(even)
    def _():
        for piece in range(PIECES):
            y_copy(piece).wait_send()

    for target in range(1, 8):

        @pl.when(has_next & (next_slot < 3) & (target >= 2 * next_slot + 1))
        def _():
            b_copy(target).wait_send()

    for target in range(0, 8, 2):

        @pl.when(has_next & ((ti != target) | (slot == 3)))
        def _():
            e_copy(target).wait_send()

    @pl.when(start_share & odd)
    def _():
        for target in range(0, 8, 2):
            start_e_copy(target).wait_send()

    @pl.when(start_share)
    def _():
        for target in range(1, 8):

            @pl.when(ti != target)
            def _():
                start_b_copy(target).wait_send()

    for d in range(1, 16):

        @pl.when(even & (tb + d < outer))
        def _():
            g_copy(d).wait_send()

    @pl.when(even)
    def _():
        state_copy(0).wait_send()

        @pl.when(slot == 3)
        def _():
            state_copy(1).wait_send()

    @pl.when(odd & jnp.logical_not(last_interval))
    def _():
        for piece in range(len(C_PIECES)):
            for target in range(2):
                c_copy(piece, target).wait_send()

    for index in range(2):
        for copy in out_copies(index):
            copy.wait()


def shards(sources, initial_state, roughness, region_ids, diffusion_table, velocity_table):
    vmem, sems = pltpu.VMEM, pltpu.SemaphoreType.DMA
    scratch = dict(
        raw=vmem((4, 4, 256, 128), F32),
        ids_raw=vmem((16, 16), jnp.int32),
        diffusion_entries=pltpu.SMEM((16,), F32),
        velocity_entries=pltpu.SMEM((2, 16), F32),
        maps=vmem((48, 512), F32),
        ids_wide=vmem((16, 128), jnp.int32),
        coef0=vmem((5, 32, 8, 512), F32),
        coef1=vmem((5, 16, 8, 256), F32),
        coef2=vmem((5, 8, 8, 128), F32),
        down1=vmem((512, 256), BF16),
        down2=vmem((256, 128), BF16),
        up1=vmem((128, 256), BF16),
        up0=vmem((256, 512), BF16),
        rhs=vmem((2, 34, 8, 512), F32),
        y=vmem((34, 8, 512), F32),
        work=vmem((2, 34, 8, 512), F32),
        tmid=vmem((32, 8, 512), F32),
        c_own=vmem((32, 8, 512), F32),
        y_in=vmem((34, 8, 512), F32),
        c_in=vmem((32, 8, 512), F32),
        third=vmem((32, 8, 512), F32),
        beta=vmem((16, 8, 256), F32),
        swap_in=vmem((8, 8, 256), F32),
        b_own=vmem((8, 8, 256), F32),
        b_in=vmem((3, 16, 8, 256), F32),
        mid=vmem((16, 8, 256), F32),
        mid_own=vmem((16, 8, 256), F32),
        level1=vmem((2, 18, 8, 256), F32),
        e_own=vmem((8, 8, 128), F32),
        e_in=vmem((8, 8, 8, 128), F32),
        g_own=vmem((8, 8, 128), F32),
        g_in=vmem((16, 8, 8, 128), F32),
        out_raw=vmem((2, 4, 256, 128), F32),
        in_sem=sems((4, 4)),
        small_sem=sems((3,)),
        out_sem=sems((2, 4)),
        y_send=sems((PIECES,)),
        y_recv=sems((PIECES,)),
        c_send=sems((2 * len(C_PIECES),)),
        c_recv=sems((len(C_PIECES),)),
        s_send=sems(()),
        s_recv=sems(()),
        b_send=sems((8,)),
        b_recv=sems((6,)),
        e_send=sems((8,)),
        e_recv=sems((8,)),
        g_send=sems((16,)),
        g_recv=sems((16,)),
        start_beta=vmem((16, 8, 256), F32),
        start_e=vmem((8, 8, 128), F32),
        start_e_send=sems((8,)),
        start_b_send=sems((8,)),
        ready_far=pltpu.SemaphoreType.REGULAR,
        ready_all=pltpu.SemaphoreType.REGULAR,
        states=vmem((2, 8, 8, 128), F32),
        w_send=sems((2,)),
        w_recv=sems((2,)),
    )
    anywhere = pl.BlockSpec(memory_space=pl.ANY)
    return pl.pallas_call(
        kernel,
        out_shape=pltpu.VMEM(sources.shape, F32),
        in_specs=[pl.BlockSpec(memory_space=pltpu.HBM)] * 6,
        out_specs=anywhere,
        scratch_shapes=list(scratch.values()),
        compiler_params=pltpu.CompilerParams(
            collective_id=0, has_side_effects=True, vmem_limit_bytes=60 * 1024 * 1024
        ),
    )(sources, initial_state, roughness, region_ids, diffusion_table, velocity_table.T)


def solution(mesh):
    in_specs = (P(("tb", "ti"), None, None), P(), P(), P(), P(), P())
    out_specs = P(("tb", "ti"), None, None)
    return jax.shard_map(shards, mesh=mesh, in_specs=in_specs, out_specs=out_specs, check_vma=False)
```
